32 devices in a mesh: tm: 4 (over x, core), space: 8 (over z, y).
Axes of the slice: x: 2, y: 2, z: 4, core: 2. Of those that a mesh axis runs over, the one named last changes fastest.
Arguments:
- queries: bfloat16 [4, 8, 2, 256, 1536], P('tm', 'space'), may hold values from -8 to 8
- keys: bfloat16 [4, 8, 2, 256, 1536], P('tm', 'space'), may hold values from -6 to 6
- values: bfloat16 [4, 8, 2, 256, 1536], P('tm', 'space'), may hold values from -6 to 6
- tile_mask: int32 [4, 8, 2, 27], P('tm', 'space'), may hold values 0 or 1
- head_reach: int32 [12, 3], replicated, may hold values from 0 to 1, as said below
Outputs:
- attended: bfloat16 [4, 8, 2, 256, 1536], P('tm', 'space')
The draws below stay inside these ranges and needn't reach their ends.
Inputs may be any that keep to these rules, and one draw needn't show every extreme that they name: `head_reach`: some head has reach 1 along all three dimensions.
All inputs are finite; a program needn't handle non-finite values. No bound on the sum of `tile_mask` on one device may be relied on, other than what follows from the above.
Results may differ from the reference program's by a relative error of at most 0.0034.
Values may be sent and summed in bfloat16 or wider, within the bound.
A program may use at most 320 MiB of HBM per device.

```python
import jax
import jax.numpy as jnp
from jax import lax

HEADS = 12
HD = 128
NWT = 2
TILE = 256
NFT = 4
NHT = 8


def draw_queries(key, part):
    shape = (NFT, NHT, NWT, TILE, HEADS * HD)
    own_key = jax.random.fold_in(key, 1)
    result = jnp.clip(2.0 * jax.random.normal(own_key, shape, jnp.float32), -8.0, 8.0)
    return result.astype(jnp.bfloat16)


def draw_keys(key, part):
    shape = (NFT, NHT, NWT, TILE, HEADS * HD)
    own_key = jax.random.fold_in(key, 2)
    result = jnp.clip(jax.random.normal(own_key, shape, jnp.float32), -6.0, 6.0)
    return result.astype(jnp.bfloat16)


def draw_head_reach(key, part):
    reach = jax.random.randint(jax.random.fold_in(key, 3), (HEADS, 3), 0, 2, dtype=jnp.int32)
    chosen = jax.random.randint(jax.random.fold_in(key, 4), (), 0, HEADS, dtype=jnp.int32)
    full = (jnp.arange(HEADS, dtype=jnp.int32) == chosen).astype(jnp.int32)[:, None]
    return jnp.maximum(reach, full)


def plant(array, key, least, high):
    longest = array.shape.index(max(array.shape))
    spots = []
    for shift in (0, 1):
        where = [jax.random.randint(jax.random.fold_in(key, axis), (), 0, length) for axis, length in enumerate(array.shape)]
        where[longest] = (where[longest] + shift) % array.shape[longest]
        spots.append(tuple(where))
    return array.at[spots[0]].set(least).at[spots[1]].set(high)


def shard_levels(key, shape, shards, low, high):
    gain = 1.0
    for dim, shards_of in shards:
        heights = jax.random.uniform(jax.random.fold_in(jax.random.fold_in(key, 6), dim), (shards_of,), jnp.float32, low / len(shards), high / len(shards))
        gain = gain * jnp.repeat(jnp.exp(heights), shape[dim] // shards_of).reshape((-1,) + (1,) * (len(shape) - 1 - dim))
    return gain


def scatter_about(stream_key, shape, spread, most, shards=(), kind=jnp.bfloat16):
    level = shard_levels(stream_key, shape, shards, -0.22, 0.18) if shards else 1.0
    values = jax.random.normal(stream_key, shape, jnp.float32) * spread * level
    return jnp.minimum(jnp.maximum(values, -most), most).astype(kind)


def setup_inputs(seed: int = 0) -> dict:
    streams_of = jax.random.split(jax.random.key(seed), 6)
    queries = draw_queries(jax.random.fold_in(streams_of[5], 71), 0)
    keys = draw_keys(jax.random.fold_in(streams_of[5], 71), 0)
    values = scatter_about(streams_of[2], (NFT, NHT, NWT, TILE, HEADS * HD), 1.0, 6.0, ((0, 4), (1, 8)))
    tile_mask = plant((jax.random.randint(streams_of[3], (NFT, NHT, NWT, 27), 0, 4) < 3).astype(jnp.int32), jax.random.fold_in(streams_of[3], 1), 0, 1)
    head_reach = draw_head_reach(jax.random.fold_in(streams_of[5], 71), 0)
    return dict(queries=queries, keys=keys, values=values, tile_mask=tile_mask, head_reach=head_reach)


def tile_allow(mask_row, reach, frame_pos, height_pos, width_pos, frame_count, height_count, width_count):
    shift = jnp.arange(3, dtype=jnp.int32) - 1
    frame_step = shift[:, None, None]
    height_step = shift[None, :, None]
    width_step = shift[None, None, :]
    inside = (frame_pos + frame_step >= 0) & (frame_pos + frame_step < frame_count)
    inside = inside & (height_pos + height_step >= 0) & (height_pos + height_step < height_count)
    inside = inside & (width_pos + width_step >= 0) & (width_pos + width_step < width_count)
    picked = mask_row.reshape(3, 3, 3)
    center = (frame_step == 0) & (height_step == 0) & (width_step == 0)
    tile_ok = inside & ((picked == 1) | center)
    within = jnp.abs(frame_step)[None] <= reach[:, 0, None, None, None]
    within = within & (jnp.abs(height_step)[None] <= reach[:, 1, None, None, None])
    within = within & (jnp.abs(width_step)[None] <= reach[:, 2, None, None, None])
    return tile_ok[None] & within


def attend(query_tile, key_rows, value_rows, allow):
    heads = allow.shape[0]
    tile_len = query_tile.shape[0]
    token_allow = jnp.repeat(allow.reshape(heads, -1), tile_len, axis=1)
    highest = lax.Precision.HIGHEST

    def per_head(head):
        query_head = lax.dynamic_slice_in_dim(query_tile, head * HD, HD, 1).astype(jnp.float32)
        key_head = lax.dynamic_slice_in_dim(key_rows, head * HD, HD, 1).astype(jnp.float32)
        value_head = lax.dynamic_slice_in_dim(value_rows, head * HD, HD, 1).astype(jnp.float32)
        usable = token_allow[head]
        scores = jnp.dot(query_head, key_head.T, precision=highest) * (HD ** -0.5)
        scores = jnp.where(usable[None, :], scores, jnp.float32(-1e30))
        largest = jnp.max(scores, axis=1, keepdims=True)
        weights = jnp.where(usable[None, :], jnp.exp(scores - largest), jnp.float32(0.0))
        totals = jnp.sum(weights, axis=1, keepdims=True)
        rounded = weights.astype(jnp.bfloat16).astype(jnp.float32)
        return jnp.dot(rounded, value_head, precision=highest) / totals

    result = lax.map(per_head, jnp.arange(heads, dtype=jnp.int32))
    return jnp.transpose(result, (1, 0, 2)).reshape(tile_len, heads * HD).astype(jnp.bfloat16)


def reference(queries, keys, values, tile_mask, head_reach):
    frame_count, height_count, width_count, tile_len, width = queries.shape
    padding = ((1, 1), (1, 1), (1, 1), (0, 0), (0, 0))
    key_pad = jnp.pad(keys, padding)
    value_pad = jnp.pad(values, padding)
    plane_count = height_count * width_count

    def one_tile(index):
        frame_pos = index // plane_count
        plane_pos = index % plane_count
        height_pos = plane_pos // width_count
        width_pos = plane_pos % width_count
        zero = jnp.int32(0)
        start = (frame_pos, height_pos, width_pos, zero, zero)
        key_rows = lax.dynamic_slice(key_pad, start, (3, 3, 3, tile_len, width)).reshape(-1, width)
        value_rows = lax.dynamic_slice(value_pad, start, (3, 3, 3, tile_len, width)).reshape(-1, width)
        query_tile = lax.dynamic_slice(queries, start, (1, 1, 1, tile_len, width)).reshape(tile_len, width)
        mask_row = lax.dynamic_slice(tile_mask, (frame_pos, height_pos, width_pos, zero), (1, 1, 1, 27)).reshape(27)
        allow = tile_allow(mask_row, head_reach, frame_pos, height_pos, width_pos, frame_count, height_count, width_count)
        return attend(query_tile, key_rows, value_rows, allow)

    result = lax.map(one_tile, jnp.arange(frame_count * plane_count, dtype=jnp.int32))
    return result.reshape(frame_count, height_count, width_count, tile_len, width)
```

```python
import functools

import jax
import jax.numpy as jnp
import numpy as np
from jax import lax
from jax.experimental import pallas as pl
from jax.experimental.pallas import tpu as pltpu
from jax.sharding import PartitionSpec as P

HD = 128
EXPONENT = float(np.log2(np.e) * HD**-0.5)
SLOTS = 9
FRAME_SLOTS = (1, 4, 7)
TILES = 18
ROW = 1 + 2 + SLOTS + 2 * TILES
PARTS = {
    1: (1,),
    2: (1, 1),
    3: (1, 1, 1),
    4: (2, 1, 1),
    5: (2, 2, 1),
    6: (3, 2, 1),
    7: (3, 2, 2),
    8: (4, 2, 2),
    9: (4, 3, 2),
    10: (5, 3, 2),
    12: (6, 4, 2),
}
COUNTS = (2, 4, 5, 6, 7, 8, 10, 12)


def passed_along(value, axis, by):
    count = lax.axis_size(axis)
    pairs = [(i, i + by) for i in range(count) if 0 <= i + by < count]
    return lax.ppermute(value, axis, pairs)


def head_order(reach):
    heads = reach.shape[0]
    frame, height = reach[:, 0] > 0, reach[:, 1] > 0
    group = jnp.where(height, jnp.where(frame, 1, 2), jnp.where(frame, 0, 3))
    place = group * heads + jnp.arange(heads, dtype=jnp.int32)
    rank = jnp.sum((place[None, :] < place[:, None]).astype(jnp.int32), axis=1)
    ids = jnp.arange(heads, dtype=jnp.int32)
    order = jnp.sum(jnp.where(rank[:, None] == ids[None, :], ids[:, None], 0), axis=0)
    only_frame = jnp.sum((group == 0).astype(jnp.int32))
    with_height = jnp.sum(height.astype(jnp.int32))
    return order, only_frame, with_height


def plan(mask, reach, order, frame_pos, height_pos, frame_count, height_count):
    heads = reach.shape[0]
    tile = np.arange(TILES, dtype=np.int32)
    frame, height = tile // 6 - 1, tile // 2 % 3 - 1
    wide = tile % 2 - np.arange(2, dtype=np.int32)[:, None]
    offset = 9 * (frame + 1) + 3 * (height + 1) + wide + 1
    chosen = (offset[:, :, None] == np.arange(27)).astype(np.int32)
    center = offset == 13
    inside = (frame_pos + frame >= 0) & (frame_pos + frame < frame_count)
    inside = inside & (height_pos + height >= 0) & (height_pos + height < height_count)
    picked = jnp.sum(mask[:, None, :] * chosen, axis=2)
    tile_ok = inside[None, :] & ((picked == 1) | center)
    sorted_reach = reach[order]
    within = np.abs(frame) <= sorted_reach[:, 0:1]
    within = within & (np.abs(height) <= sorted_reach[:, 1:2])
    allow = (
        tile_ok[None] & within[:, None] & (np.abs(wide) <= sorted_reach[:, 2][:, None, None])
    )
    in_slot = (tile // 2 == np.arange(SLOTS)[:, None]).astype(np.int32)
    used = jnp.sum(allow.astype(jnp.int32), axis=1)
    need = (jnp.sum(used[:, None, :] * in_slot, axis=2) > 0).astype(jnp.int32)
    ahead = np.tril(np.ones((TILES, TILES), np.int32), -1)
    place = jnp.sum(allow[:, :, None, :].astype(jnp.int32) * ahead, axis=3)
    ids = tile
    hit = allow[:, :, :, None] & (place[:, :, :, None] == ids)
    tiles = jnp.sum(jnp.where(hit, ids[:, None], 0), axis=2)
    counts = jnp.sum(allow.astype(jnp.int32), axis=2)
    tiles = jnp.where(ids < counts[:, :, None], tiles, tiles[:, :, 0:1])
    rows = [order[:, None], counts, need, tiles.reshape(heads, 2 * TILES)]
    return jnp.concatenate(rows, axis=1).reshape(-1)


def pack_kernel(order_ref, key_ref, value_ref, out_ref):
    out_ref[0, 0] = key_ref[0, 0]
    out_ref[0, 1] = value_ref[0, 0]


def packed(order, keys, values):
    heads = order.shape[0]
    tile_len = keys.shape[3]
    block = pl.BlockSpec((1, 1, 2, tile_len, HD), lambda i, order: (0, 0, 0, 0, order[i]))
    return pl.pallas_call(
        pack_kernel,
        out_shape=jax.ShapeDtypeStruct((heads, 2, 2, tile_len, HD), keys.dtype),
        grid_spec=pltpu.PrefetchScalarGridSpec(
            num_scalar_prefetch=1,
            grid=(heads,),
            in_specs=[block, block],
            out_specs=pl.BlockSpec(
                (1, 2, 2, tile_len, HD), lambda i, order: (i, 0, 0, 0, 0)
            ),
        ),
    )(order, keys, values)


def attend_kernel(count, heads, tile_len, sources, aliased, base_ref, plan_ref, q_ref, *refs):
    pieces = refs[: len(sources)]
    out_ref, kv, scores, sems = refs[len(sources) + int(aliased) :]
    i = pl.program_id(0)
    contract = (((1,), (1,)), ((), ()))

    def place_of(step):
        return lax.rem(base_ref[0] + step, heads)

    def transfer(step, buf, begin):
        place = place_of(step)
        for ref, (slot, local) in zip(pieces, sources):

            @pl.when(plan_ref[place * ROW + 3 + slot] > 0)
            def _():
                copy = pltpu.make_async_copy(
                    ref.at[step if local else place], kv.at[buf, slot], sems.at[buf, slot]
                )
                if begin:
                    copy.start()
                else:
                    copy.wait()

    @pl.when(i == 0)
    def _():
        transfer(i, 0, True)

    buf = lax.rem(i, 2)

    @pl.when(i + 1 < count)
    def _():
        transfer(i + 1, 1 - buf, True)

    transfer(i, buf, False)
    row = place_of(i) * ROW

    def column(c, carry):
        query = q_ref[0, 0, c]
        tiles = plan_ref[row + 1 + c]
        first = row + 3 + SLOTS + c * TILES

        def score(p, largest):
            a, b = plan_ref[first + 2 * p], plan_ref[first + 2 * p + 1]
            low = lax.dot_general(
                query, kv[buf, a // 2, 0, a % 2], contract, preferred_element_type=jnp.float32
            )
            high = lax.dot_general(
                query, kv[buf, b // 2, 0, b % 2], contract, preferred_element_type=jnp.float32
            )
            high = jnp.where(2 * p + 1 < tiles, high, jnp.float32(-1e30))
            scores[p, :, :tile_len] = low
            scores[p, :, tile_len:] = high
            for part in (low, high):
                for k in range(0, tile_len, HD):
                    largest = jnp.maximum(largest, part[:, k : k + HD])
            return largest

        pairs = (tiles + 1) // 2
        largest = lax.fori_loop(
            0, pairs, score, jnp.full((tile_len, HD), -jnp.inf, jnp.float32)
        )
        largest = jnp.max(largest, axis=1, keepdims=True)

        def gather(p, state):
            total, result = state
            a, b = plan_ref[first + 2 * p], plan_ref[first + 2 * p + 1]
            for at, tile in ((0, a), (tile_len, b)):
                part = scores[p, :, at : at + tile_len]
                weights = jnp.exp2((part - largest) * EXPONENT)
                for k in range(0, tile_len, HD):
                    total = total + weights[:, k : k + HD]
                result = result + jnp.dot(
                    weights.astype(jnp.bfloat16),
                    kv[buf, tile // 2, 1, tile % 2],
                    preferred_element_type=jnp.float32,
                )
            return total, result

        zero = jnp.zeros((tile_len, HD), jnp.float32)
        total, result = lax.fori_loop(0, pairs, gather, (zero, zero))
        total = jnp.sum(total, axis=1, keepdims=True)
        out_ref[0, 0, c] = (result / total).astype(jnp.bfloat16)
        return carry

    lax.fori_loop(0, 2, column, 0)


def attend(base, table, queries, pieces, count, heads, out):
    tile_len = queries.shape[3]
    block = pl.BlockSpec(
        (1, 1, 2, tile_len, HD),
        lambda i, base, table: (0, 0, 0, 0, table[lax.rem(base[0] + i, heads) * ROW]),
    )
    anywhere = pl.BlockSpec(memory_space=pl.ANY)
    arrays = [array for _, _, array in pieces]
    sources = tuple((slot, local) for slot, local, _ in pieces)
    aliased = out is not None
    extra = [out] if aliased else []
    work = count * 2 * tile_len * TILES * tile_len // 3
    return pl.pallas_call(
        functools.partial(attend_kernel, count, heads, tile_len, sources, aliased),
        out_shape=jax.ShapeDtypeStruct(queries.shape, queries.dtype),
        grid_spec=pltpu.PrefetchScalarGridSpec(
            num_scalar_prefetch=2,
            grid=(count,),
            in_specs=[block] + [anywhere] * (len(arrays) + len(extra)),
            out_specs=block,
            scratch_shapes=[
                pltpu.VMEM((2, SLOTS, 2, 2, tile_len, HD), queries.dtype),
                pltpu.VMEM((TILES // 2, tile_len, 2 * tile_len), jnp.float32),
                pltpu.SemaphoreType.DMA((2, SLOTS)),
            ],
        ),
        input_output_aliases={3 + len(arrays): 0} if aliased else {},
        compiler_params=pltpu.CompilerParams(vmem_limit_bytes=32 * 1024 * 1024),
        cost_estimate=pl.CostEstimate(
            flops=work * 4 * HD, bytes_accessed=count * 2 * 1024 * 1024, transcendentals=work
        ),
    )(base, table, queries, *arrays, *extra)


def branch(reached, table, queries, own, only_frame):
    heads = own.shape[0]
    start = jnp.minimum(only_frame, heads - reached)
    before = passed_along(own, "tm", 1)
    after = passed_along(own, "tm", -1)
    frames = [(1, False, before), (4, False, own), (7, False, after)]
    received, at = [], 0
    for size in PARTS[reached]:
        part = lax.dynamic_slice_in_dim(own, start + at, size, 0)
        pieces = []
        for slot, by in ((3, 1), (5, -1)):
            side = passed_along(part, "space", by)
            pieces.append((slot, True, side))
            pieces.append((slot - 3, True, passed_along(side, "tm", 1)))
            pieces.append((slot + 3, True, passed_along(side, "tm", -1)))
        received.append((at, size, pieces))
        at += size
    out = None
    if reached < heads:
        base = (start + reached).reshape(1)
        out = attend(base, table, queries, frames, heads - reached, heads, out)
    for at, size, pieces in received:
        base = (start + at).reshape(1)
        out = attend(base, table, queries, frames + pieces, size, heads, out)
    return out


def local(queries, keys, values, tile_mask, head_reach):
    order, only_frame, with_height = head_order(head_reach)
    own = packed(order, keys, values)
    table = plan(
        tile_mask[0, 0],
        head_reach,
        order,
        lax.axis_index("tm"),
        lax.axis_index("space"),
        lax.axis_size("tm"),
        lax.axis_size("space"),
    )
    which = jnp.sum((with_height > np.array(COUNTS, np.int32)).astype(jnp.int32))
    branches = [functools.partial(branch, count) for count in COUNTS]
    return lax.switch(which, branches, table, queries, own, only_frame)


def solution(mesh):
    in_specs = (
        P("tm", "space", None, None, None),
        P("tm", "space", None, None, None),
        P("tm", "space", None, None, None),
        P("tm", "space", None, None),
        P(),
    )
    out_specs = P("tm", "space", None, None, None)
    return jax.shard_map(local, mesh=mesh, in_specs=in_specs, out_specs=out_specs, check_vma=False)
```

```python
import functools

import jax
import jax.numpy as jnp
import numpy as np
from jax import lax
from jax.experimental import pallas as pl
from jax.experimental.pallas import tpu as pltpu
from jax.sharding import PartitionSpec as P

HD = 128
EXPONENT = float(np.log2(np.e) * HD**-0.5)
SLOTS = 9
FRAME_SLOTS = (1, 4, 7)
TILES = 18
ROW = 1 + 2 + SLOTS + 2 * TILES
WINDOW = 3
COUNTS = (2, 4, 5, 6, 7, 8, 10, 12)


def head_order(reach):
    heads = reach.shape[0]
    frame, height = reach[:, 0] > 0, reach[:, 1] > 0
    group = jnp.where(height, 0, 2) + jnp.where(frame, 0, 1)
    place = group * heads + jnp.arange(heads, dtype=jnp.int32)
    rank = jnp.sum((place[None, :] < place[:, None]).astype(jnp.int32), axis=1)
    ids = jnp.arange(heads, dtype=jnp.int32)
    order = jnp.sum(jnp.where(rank[:, None] == ids[None, :], ids[:, None], 0), axis=0)
    with_height = jnp.sum(height.astype(jnp.int32))
    return order, with_height


def plan(mask, reach, order, frame_pos, height_pos, frame_count, height_count):
    heads = reach.shape[0]
    tile = np.arange(TILES, dtype=np.int32)
    frame, height = tile // 6 - 1, tile // 2 % 3 - 1
    wide = tile % 2 - np.arange(2, dtype=np.int32)[:, None]
    offset = 9 * (frame + 1) + 3 * (height + 1) + wide + 1
    chosen = (offset[:, :, None] == np.arange(27)).astype(np.int32)
    center = offset == 13
    inside = (frame_pos + frame >= 0) & (frame_pos + frame < frame_count)
    inside = inside & (height_pos + height >= 0) & (height_pos + height < height_count)
    picked = jnp.sum(mask[:, None, :] * chosen, axis=2)
    tile_ok = inside[None, :] & ((picked == 1) | center)
    sorted_reach = reach[order]
    within = np.abs(frame) <= sorted_reach[:, 0:1]
    within = within & (np.abs(height) <= sorted_reach[:, 1:2])
    allow = (
        tile_ok[None] & within[:, None] & (np.abs(wide) <= sorted_reach[:, 2][:, None, None])
    )
    in_slot = (tile // 2 == np.arange(SLOTS)[:, None]).astype(np.int32)
    used = jnp.sum(allow.astype(jnp.int32), axis=1)
    need = (jnp.sum(used[:, None, :] * in_slot, axis=2) > 0).astype(jnp.int32)
    ahead = np.tril(np.ones((TILES, TILES), np.int32), -1)
    place = jnp.sum(allow[:, :, None, :].astype(jnp.int32) * ahead, axis=3)
    ids = tile
    hit = allow[:, :, :, None] & (place[:, :, :, None] == ids)
    tiles = jnp.sum(jnp.where(hit, ids[:, None], 0), axis=2)
    counts = jnp.sum(allow.astype(jnp.int32), axis=2)
    tiles = jnp.where(ids < counts[:, :, None], tiles, tiles[:, :, 0:1])
    rows = [order[:, None], counts, need, tiles.reshape(heads, 2 * TILES)]
    return jnp.concatenate(rows, axis=1).reshape(-1)


def pack_kernel(heads, order_ref, key_ref, value_ref, out_ref, sems):
    def copies(head):
        columns = pl.ds(pl.multiple_of(order_ref[head] * HD, HD), HD)
        return [
            pltpu.make_async_copy(
                ref.at[0, 0, :, :, columns], out_ref.at[head, kind], sems.at[kind, head]
            )
            for kind, ref in enumerate((key_ref, value_ref))
        ]

    def begin(head, carry):
        for copy in copies(head):
            copy.start()
        return carry

    def finish(head, carry):
        for copy in copies(head):
            copy.wait()
        return carry

    lax.fori_loop(0, heads, begin, 0)
    lax.fori_loop(0, heads, finish, 0)


def packed(order, keys, values):
    heads = order.shape[0]
    tile_len = keys.shape[3]
    anywhere = pl.BlockSpec(memory_space=pl.ANY)
    return pl.pallas_call(
        functools.partial(pack_kernel, heads),
        out_shape=jax.ShapeDtypeStruct((heads, 2, 2, tile_len, HD), keys.dtype),
        grid_spec=pltpu.PrefetchScalarGridSpec(
            num_scalar_prefetch=1,
            grid=(),
            in_specs=[anywhere, anywhere],
            out_specs=anywhere,
            scratch_shapes=[pltpu.SemaphoreType.DMA((2, heads))],
        ),
    )(order, keys, values)


def exchange_kernel(
    reached,
    frame_count,
    height_count,
    own,
    before,
    after,
    above,
    below,
    above_before,
    above_after,
    below_before,
    below_after,
    frame_send,
    frame_recv,
    side_send,
    side_recv,
    relay_send,
    relay_recv,
):
    frame, height = lax.axis_index("tm"), lax.axis_index("space")
    has_prev, has_next = frame > 0, frame < frame_count - 1
    has_above, has_below = height > 0, height < height_count - 1
    prev, following = (frame - 1, height), (frame + 1, height)
    upper, lower = (frame, height - 1), (frame, height + 1)
    mesh_id = pl.DeviceIdType.MESH
    neighbours = (
        (has_prev, prev),
        (has_next, following),
        (has_above, upper),
        (has_below, lower),
    )

    barrier = pltpu.get_barrier_semaphore()
    for there, device in neighbours:

        @pl.when(there)
        def _():
            pl.semaphore_signal(barrier, inc=1, device_id=device, device_id_type=mesh_id)

    peers = sum(there.astype(jnp.int32) for there, _ in neighbours)
    pl.semaphore_wait(barrier, peers)

    def remote(src, dst, send, recv, device):
        return pltpu.make_async_remote_copy(
            src_ref=src,
            dst_ref=dst,
            send_sem=send,
            recv_sem=recv,
            device_id=device,
            device_id_type=mesh_id,
        )

    def frame_copies():
        return (
            (has_next, has_prev, remote(own, before, frame_send.at[0], frame_recv.at[0], following)),
            (has_prev, has_next, remote(own, after, frame_send.at[1], frame_recv.at[1], prev)),
        )

    def side_copies(j):
        down = remote(own.at[j], above.at[j], side_send.at[0, j], side_recv.at[0, j], lower)
        up = remote(own.at[j], below.at[j], side_send.at[1, j], side_recv.at[1, j], upper)
        return (has_below, has_above, down), (has_above, has_below, up)

    def relay_copies(j):
        made = []
        for k, (src, dst, there, send_to) in enumerate(
            (
                (above, above_before, has_above, True),
                (above, above_after, has_above, False),
                (below, below_before, has_below, True),
                (below, below_after, has_below, False),
            )
        ):
            device = following if send_to else prev
            sends = has_next if send_to else has_prev
            receives = has_prev if send_to else has_next
            copy = remote(src.at[j], dst.at[j], relay_send.at[k, j], relay_recv.at[k, j], device)
            made.append((there & sends, there & receives, copy))
        return made

    def start(copies):
        for sends, _, copy in copies:

            @pl.when(sends)
            def _():
                copy.start()

    def wait_sent(copies):
        for sends, _, copy in copies:

            @pl.when(sends)
            def _():
                copy.wait_send()

    def wait_received(copies):
        for _, receives, copy in copies:

            @pl.when(receives)
            def _():
                copy.wait_recv()

    for j in range(min(WINDOW, reached)):
        start(side_copies(j))
    start(frame_copies())

    def step(j, carry):
        wait_sent(side_copies(j))

        @pl.when(j + WINDOW < reached)
        def _():
            start(side_copies(jnp.minimum(j + WINDOW, reached - 1)))

        wait_received(side_copies(j))
        start(relay_copies(j))
        return carry

    lax.fori_loop(0, reached, step, 0)

    def finish(j, carry):
        wait_sent(relay_copies(j))
        wait_received(relay_copies(j))
        return carry

    wait_sent(frame_copies())
    wait_received(frame_copies())
    lax.fori_loop(0, reached, finish, 0)


def exchanged(reached, own):
    heads = own.shape[0]
    anywhere = pl.BlockSpec(memory_space=pl.ANY)
    full = jax.ShapeDtypeStruct(own.shape, own.dtype)
    some = jax.ShapeDtypeStruct((reached,) + own.shape[1:], own.dtype)
    dma = pltpu.SemaphoreType.DMA
    return pl.pallas_call(
        functools.partial(
            exchange_kernel, reached, lax.axis_size("tm"), lax.axis_size("space")
        ),
        out_shape=[full] * 2 + [some] * 6,
        in_specs=[anywhere],
        out_specs=[anywhere] * 8,
        scratch_shapes=[
            dma((2,)),
            dma((2,)),
            dma((2, reached)),
            dma((2, reached)),
            dma((4, reached)),
            dma((4, reached)),
        ],
        compiler_params=pltpu.CompilerParams(collective_id=reached, has_side_effects=True),
    )(own)


def attend_kernel(heads, tile_len, slots, plan_ref, q_ref, *refs):
    pieces = refs[: len(slots)]
    out_ref, kv, scores, peak, sems = refs[len(slots) :]
    i = pl.program_id(0)
    contract = (((1,), (1,)), ((), ()))

    def transfer(place, buf, begin):
        for ref, slot in zip(pieces, slots):

            @pl.when(plan_ref[place * ROW + 3 + slot] > 0)
            def _():
                copy = pltpu.make_async_copy(
                    ref.at[place], kv.at[buf, slot], sems.at[buf, slot]
                )
                if begin:
                    copy.start()
                else:
                    copy.wait()

    @pl.when(i == 0)
    def _():
        transfer(i, 0, True)

    buf = lax.rem(i, 2)

    @pl.when(i + 1 < heads)
    def _():
        transfer(i + 1, 1 - buf, True)

    transfer(i, buf, False)
    row = i * ROW

    def column(c, carry):
        query = q_ref[0, 0, c]
        tiles = plan_ref[row + 1 + c]
        first = row + 3 + SLOTS + c * TILES

        def score(p, largest):
            a, b = plan_ref[first + 2 * p], plan_ref[first + 2 * p + 1]
            low = lax.dot_general(
                query, kv[buf, a // 2, 0, a % 2], contract, preferred_element_type=jnp.float32
            )
            high = lax.dot_general(
                query, kv[buf, b // 2, 0, b % 2], contract, preferred_element_type=jnp.float32
            )
            high = jnp.where(2 * p + 1 < tiles, high, jnp.float32(-1e30))
            scores[p, :, :tile_len] = low
            scores[p, :, tile_len:] = high
            for part in (low, high):
                for k in range(0, tile_len, HD):
                    largest = jnp.maximum(largest, part[:, k : k + HD])
            return largest

        pairs = (tiles + 1) // 2
        largest = lax.fori_loop(
            0, pairs, score, jnp.full((tile_len, HD), -jnp.inf, jnp.float32)
        )
        largest = jnp.max(largest, axis=1, keepdims=True)
        peak[...] = jnp.broadcast_to(largest, (tile_len, HD))

        def gather(p, state):
            total, result = state
            a, b = plan_ref[first + 2 * p], plan_ref[first + 2 * p + 1]
            for at, tile in ((0, a), (tile_len, b)):
                rounded = []
                for k in range(at, at + tile_len, HD):
                    weights = jnp.exp2((scores[p, :, k : k + HD] - peak[...]) * EXPONENT)
                    total = total + weights
                    rounded.append(weights.astype(jnp.bfloat16))
                result = result + jnp.dot(
                    jnp.concatenate(rounded, axis=1),
                    kv[buf, tile // 2, 1, tile % 2],
                    preferred_element_type=jnp.float32,
                )
            return total, result

        zero = jnp.zeros((tile_len, HD), jnp.float32)
        total, result = lax.fori_loop(0, pairs, gather, (zero, zero))
        total = jnp.sum(total, axis=1, keepdims=True)
        out_ref[0, 0, c] = (result / total).astype(jnp.bfloat16)
        return carry

    lax.fori_loop(0, 2, column, 0)


def attend(table, queries, pieces, heads):
    tile_len = queries.shape[3]
    block = pl.BlockSpec(
        (1, 1, 2, tile_len, HD), lambda i, table: (0, 0, 0, 0, table[i * ROW])
    )
    anywhere = pl.BlockSpec(memory_space=pl.ANY)
    arrays = [array for _, array in pieces]
    slots = tuple(slot for slot, _ in pieces)
    work = heads * 2 * tile_len * TILES * tile_len // 3
    return pl.pallas_call(
        functools.partial(attend_kernel, heads, tile_len, slots),
        out_shape=jax.ShapeDtypeStruct(queries.shape, queries.dtype),
        grid_spec=pltpu.PrefetchScalarGridSpec(
            num_scalar_prefetch=1,
            grid=(heads,),
            in_specs=[block] + [anywhere] * len(arrays),
            out_specs=block,
            scratch_shapes=[
                pltpu.VMEM((2, SLOTS, 2, 2, tile_len, HD), queries.dtype),
                pltpu.VMEM((TILES // 2, tile_len, 2 * tile_len), jnp.float32),
                pltpu.VMEM((tile_len, HD), jnp.float32),
                pltpu.SemaphoreType.DMA((2, SLOTS)),
            ],
        ),
        compiler_params=pltpu.CompilerParams(vmem_limit_bytes=32 * 1024 * 1024),
        cost_estimate=pl.CostEstimate(
            flops=work * 4 * HD, bytes_accessed=heads * 2 * 1024 * 1024, transcendentals=work
        ),
    )(table, queries, *arrays)


def branch(reached, table, queries, own):
    heads = own.shape[0]
    arrays = exchanged(reached, own)
    pieces = [(1, arrays[0]), (4, own), (7, arrays[1])]
    pieces += zip((3, 5, 0, 6, 2, 8), arrays[2:])
    return attend(table, queries, pieces, heads)


def local(queries, keys, values, tile_mask, head_reach):
    order, with_height = head_order(head_reach)
    own = packed(order, keys, values)
    table = plan(
        tile_mask[0, 0],
        head_reach,
        order,
        lax.axis_index("tm"),
        lax.axis_index("space"),
        lax.axis_size("tm"),
        lax.axis_size("space"),
    )
    which = jnp.sum((with_height > np.array(COUNTS, np.int32)).astype(jnp.int32))
    branches = [functools.partial(branch, count) for count in COUNTS]
    return lax.switch(which, branches, table, queries, own)


def solution(mesh):
    in_specs = (
        P("tm", "space", None, None, None),
        P("tm", "space", None, None, None),
        P("tm", "space", None, None, None),
        P("tm", "space", None, None),
        P(),
    )
    out_specs = P("tm", "space", None, None, None)
    return jax.shard_map(local, mesh=mesh, in_specs=in_specs, out_specs=out_specs, check_vma=False)
```

```python
import functools

import jax
import jax.numpy as jnp
import numpy as np
from jax import lax
from jax.experimental import pallas as pl
from jax.experimental.pallas import tpu as pltpu
from jax.sharding import PartitionSpec as P

HD = 128
EXPONENT = float(np.log2(np.e) * HD**-0.5)
SLOTS = 9
FRAME_SLOTS = (1, 4, 7)
TILES = 18
ROW = 1 + SLOTS + 2 * TILES
WINDOW = 3
COUNTS = (2, 3, 4, 5, 6, 7, 8, 9, 10, 12)


def head_order(reach):
    heads = reach.shape[0]
    frame, height = reach[:, 0] > 0, reach[:, 1] > 0
    group = jnp.where(height, 0, 2) + jnp.where(frame, 0, 1)
    place = group * heads + jnp.arange(heads, dtype=jnp.int32)
    rank = jnp.sum((place[None, :] < place[:, None]).astype(jnp.int32), axis=1)
    ids = jnp.arange(heads, dtype=jnp.int32)
    order = jnp.sum(jnp.where(rank[:, None] == ids[None, :], ids[:, None], 0), axis=0)
    with_height = jnp.sum(height.astype(jnp.int32))
    return order, with_height


def plan(mask, reach, order, frame_pos, height_pos, frame_count, height_count):
    heads = reach.shape[0]
    tile = np.arange(TILES, dtype=np.int32)
    frame, height = tile // 6 - 1, tile // 2 % 3 - 1
    wide = tile % 2 - np.arange(2, dtype=np.int32)[:, None]
    offset = 9 * (frame + 1) + 3 * (height + 1) + wide + 1
    chosen = (offset[:, :, None] == np.arange(27)).astype(np.int32)
    center = offset == 13
    inside = (frame_pos + frame >= 0) & (frame_pos + frame < frame_count)
    inside = inside & (height_pos + height >= 0) & (height_pos + height < height_count)
    picked = jnp.sum(mask[:, None, :] * chosen, axis=2)
    tile_ok = inside[None, :] & ((picked == 1) | center)
    sorted_reach = reach[order]
    within = np.abs(frame) <= sorted_reach[:, 0:1]
    within = within & (np.abs(height) <= sorted_reach[:, 1:2])
    allow = (
        tile_ok[None] & within[:, None] & (np.abs(wide) <= sorted_reach[:, 2][:, None, None])
    )
    in_slot = (tile // 2 == np.arange(SLOTS)[:, None]).astype(np.int32)
    used = jnp.sum(allow.astype(jnp.int32), axis=1)
    need = (jnp.sum(used[:, None, :] * in_slot, axis=2) > 0).astype(jnp.int32)
    flags = allow.astype(jnp.int32).reshape(heads, 2 * TILES)
    rows = [order[:, None], need, flags]
    return jnp.concatenate(rows, axis=1).reshape(-1)


def pack_kernel(heads, order_ref, key_ref, value_ref, out_ref, sems):
    def copies(head):
        columns = pl.ds(pl.multiple_of(order_ref[head] * HD, HD), HD)
        return [
            pltpu.make_async_copy(
                ref.at[0, 0, :, :, columns], out_ref.at[head, kind], sems.at[kind, head]
            )
            for kind, ref in enumerate((key_ref, value_ref))
        ]

    def begin(head, carry):
        for copy in copies(head):
            copy.start()
        return carry

    def finish(head, carry):
        for copy in copies(head):
            copy.wait()
        return carry

    lax.fori_loop(0, heads, begin, 0)
    lax.fori_loop(0, heads, finish, 0)


def packed(order, keys, values):
    heads = order.shape[0]
    tile_len = keys.shape[3]
    anywhere = pl.BlockSpec(memory_space=pl.ANY)
    return pl.pallas_call(
        functools.partial(pack_kernel, heads),
        out_shape=jax.ShapeDtypeStruct((heads, 2, 2, tile_len, HD), keys.dtype),
        grid_spec=pltpu.PrefetchScalarGridSpec(
            num_scalar_prefetch=1,
            grid=(),
            in_specs=[anywhere, anywhere],
            out_specs=anywhere,
            scratch_shapes=[pltpu.SemaphoreType.DMA((2, heads))],
        ),
    )(order, keys, values)


def exchange_kernel(
    reached,
    frame_count,
    height_count,
    own,
    before,
    after,
    above,
    below,
    above_before,
    above_after,
    below_before,
    below_after,
    frame_send,
    frame_recv,
    side_send,
    side_recv,
    relay_send,
    relay_recv,
):
    frame, height = lax.axis_index("tm"), lax.axis_index("space")
    has_prev, has_next = frame > 0, frame < frame_count - 1
    has_above, has_below = height > 0, height < height_count - 1
    prev, following = (frame - 1, height), (frame + 1, height)
    upper, lower = (frame, height - 1), (frame, height + 1)
    mesh_id = pl.DeviceIdType.MESH
    neighbours = (
        (has_prev, prev),
        (has_next, following),
        (has_above, upper),
        (has_below, lower),
    )

    barrier = pltpu.get_barrier_semaphore()
    for there, device in neighbours:

        @pl.when(there)
        def _():
            pl.semaphore_signal(barrier, inc=1, device_id=device, device_id_type=mesh_id)

    peers = sum(there.astype(jnp.int32) for there, _ in neighbours)
    pl.semaphore_wait(barrier, peers)

    def remote(src, dst, send, recv, device):
        return pltpu.make_async_remote_copy(
            src_ref=src,
            dst_ref=dst,
            send_sem=send,
            recv_sem=recv,
            device_id=device,
            device_id_type=mesh_id,
        )

    def frame_copies():
        return (
            (has_next, has_prev, remote(own, before, frame_send.at[0], frame_recv.at[0], following)),
            (has_prev, has_next, remote(own, after, frame_send.at[1], frame_recv.at[1], prev)),
        )

    def side_copies(j):
        down = remote(own.at[j], above.at[j], side_send.at[0, j], side_recv.at[0, j], lower)
        up = remote(own.at[j], below.at[j], side_send.at[1, j], side_recv.at[1, j], upper)
        return (has_below, has_above, down), (has_above, has_below, up)

    def relay_copies(j):
        made = []
        for k, (src, dst, there, send_to) in enumerate(
            (
                (above, above_before, has_above, True),
                (above, above_after, has_above, False),
                (below, below_before, has_below, True),
                (below, below_after, has_below, False),
            )
        ):
            device = following if send_to else prev
            sends = has_next if send_to else has_prev
            receives = has_prev if send_to else has_next
            copy = remote(src.at[j], dst.at[j], relay_send.at[k, j], relay_recv.at[k, j], device)
            made.append((there & sends, there & receives, copy))
        return made

    def start(copies):
        for sends, _, copy in copies:

            @pl.when(sends)
            def _():
                copy.start()

    def wait_sent(copies):
        for sends, _, copy in copies:

            @pl.when(sends)
            def _():
                copy.wait_send()

    def wait_received(copies):
        for _, receives, copy in copies:

            @pl.when(receives)
            def _():
                copy.wait_recv()

    for j in range(min(WINDOW, reached)):
        start(side_copies(j))
    start(frame_copies())

    def step(j, carry):
        wait_sent(side_copies(j))

        @pl.when(j + WINDOW < reached)
        def _():
            start(side_copies(jnp.minimum(j + WINDOW, reached - 1)))

        wait_received(side_copies(j))
        start(relay_copies(j))
        return carry

    lax.fori_loop(0, reached, step, 0)

    def finish(j, carry):
        wait_sent(relay_copies(j))
        wait_received(relay_copies(j))
        return carry

    wait_sent(frame_copies())
    wait_received(frame_copies())
    lax.fori_loop(0, reached, finish, 0)


def exchanged(reached, own):
    heads = own.shape[0]
    anywhere = pl.BlockSpec(memory_space=pl.ANY)
    full = jax.ShapeDtypeStruct(own.shape, own.dtype)
    some = jax.ShapeDtypeStruct((reached,) + own.shape[1:], own.dtype)
    dma = pltpu.SemaphoreType.DMA
    return pl.pallas_call(
        functools.partial(
            exchange_kernel, reached, lax.axis_size("tm"), lax.axis_size("space")
        ),
        out_shape=[full] * 2 + [some] * 6,
        in_specs=[anywhere],
        out_specs=[anywhere] * 8,
        scratch_shapes=[
            dma((2,)),
            dma((2,)),
            dma((2, reached)),
            dma((2, reached)),
            dma((4, reached)),
            dma((4, reached)),
        ],
        compiler_params=pltpu.CompilerParams(collective_id=reached, has_side_effects=True),
    )(own)


def attend_kernel(heads, tile_len, slots, plan_ref, q_ref, *refs):
    pieces = refs[: len(slots)]
    out_ref, kv, scores, peak, listed, sems = refs[len(slots) :]
    i = pl.program_id(0)
    contract = (((1,), (1,)), ((), ()))

    def transfer(place, buf, begin):
        for ref, slot in zip(pieces, slots):

            @pl.when(plan_ref[place * ROW + 1 + slot] > 0)
            def _():
                copy = pltpu.make_async_copy(
                    ref.at[place], kv.at[buf, slot], sems.at[buf, slot]
                )
                if begin:
                    copy.start()
                else:
                    copy.wait()

    @pl.when(i == 0)
    def _():
        transfer(i, 0, True)

    buf = lax.rem(i, 2)

    @pl.when(i + 1 < heads)
    def _():
        transfer(i + 1, 1 - buf, True)

    transfer(i, buf, False)
    row = i * ROW

    def column(c, carry):
        query = q_ref[0, 0, c]
        first = row + 1 + SLOTS + c * TILES
        tiles = jnp.int32(0)
        for tile in range(TILES):
            listed[tiles] = tile
            tiles = tiles + plan_ref[first + tile]
        listed[tiles] = listed[0]

        def score(p, largest):
            a, b = listed[2 * p], listed[2 * p + 1]
            low = lax.dot_general(
                query, kv[buf, a // 2, 0, a % 2], contract, preferred_element_type=jnp.float32
            )
            high = lax.dot_general(
                query, kv[buf, b // 2, 0, b % 2], contract, preferred_element_type=jnp.float32
            )
            high = jnp.where(2 * p + 1 < tiles, high, jnp.float32(-1e30))
            scores[p, :, :tile_len] = low
            scores[p, :, tile_len:] = high
            for part in (low, high):
                for k in range(0, tile_len, HD):
                    largest = jnp.maximum(largest, part[:, k : k + HD])
            return largest

        pairs = (tiles + 1) // 2
        largest = lax.fori_loop(
            0, pairs, score, jnp.full((tile_len, HD), -jnp.inf, jnp.float32)
        )
        largest = jnp.max(largest, axis=1, keepdims=True)
        peak[...] = jnp.broadcast_to(largest, (tile_len, HD))

        def gather(p, state):
            total, result = state
            a, b = listed[2 * p], listed[2 * p + 1]
            rounded = []
            for k in range(0, 2 * tile_len, HD):
                weights = jnp.exp2((scores[p, :, k : k + HD] - peak[...]) * EXPONENT)
                total = total + weights
                rounded.append(weights.astype(jnp.bfloat16))
            rows = [kv[buf, tile // 2, 1, tile % 2] for tile in (a, b)]
            result = result + jnp.dot(
                jnp.concatenate(rounded, axis=1),
                jnp.concatenate(rows, axis=0),
                preferred_element_type=jnp.float32,
            )
            return total, result

        zero = jnp.zeros((tile_len, HD), jnp.float32)
        total, result = lax.fori_loop(0, pairs, gather, (zero, zero))
        total = jnp.sum(total, axis=1, keepdims=True)
        out_ref[0, 0, c] = (result / total).astype(jnp.bfloat16)
        return carry

    lax.fori_loop(0, 2, column, 0)


def attend(table, queries, pieces, heads):
    tile_len = queries.shape[3]
    block = pl.BlockSpec(
        (1, 1, 2, tile_len, HD), lambda i, table: (0, 0, 0, 0, table[i * ROW])
    )
    anywhere = pl.BlockSpec(memory_space=pl.ANY)
    arrays = [array for _, array in pieces]
    slots = tuple(slot for slot, _ in pieces)
    work = heads * 2 * tile_len * TILES * tile_len // 3
    return pl.pallas_call(
        functools.partial(attend_kernel, heads, tile_len, slots),
        out_shape=jax.ShapeDtypeStruct(queries.shape, queries.dtype),
        grid_spec=pltpu.PrefetchScalarGridSpec(
            num_scalar_prefetch=1,
            grid=(heads,),
            in_specs=[block] + [anywhere] * len(arrays),
            out_specs=block,
            scratch_shapes=[
                pltpu.VMEM((2, SLOTS, 2, 2, tile_len, HD), queries.dtype),
                pltpu.VMEM((TILES // 2, tile_len, 2 * tile_len), jnp.float32),
                pltpu.VMEM((tile_len, HD), jnp.float32),
                pltpu.SMEM((TILES + 2,), jnp.int32),
                pltpu.SemaphoreType.DMA((2, SLOTS)),
            ],
        ),
        compiler_params=pltpu.CompilerParams(vmem_limit_bytes=60 * 1024 * 1024),
        cost_estimate=pl.CostEstimate(
            flops=work * 4 * HD, bytes_accessed=heads * 2 * 1024 * 1024, transcendentals=work
        ),
    )(table, queries, *arrays)


def branch(reached, table, queries, own):
    heads = own.shape[0]
    arrays = exchanged(reached, own)
    pieces = [(1, arrays[0]), (4, own), (7, arrays[1])]
    pieces += zip((3, 5, 0, 6, 2, 8), arrays[2:])
    return attend(table, queries, pieces, heads)


def local(queries, keys, values, tile_mask, head_reach):
    order, with_height = head_order(head_reach)
    own = packed(order, keys, values)
    table = plan(
        tile_mask[0, 0],
        head_reach,
        order,
        lax.axis_index("tm"),
        lax.axis_index("space"),
        lax.axis_size("tm"),
        lax.axis_size("space"),
    )
    which = jnp.sum((with_height > np.array(COUNTS, np.int32)).astype(jnp.int32))
    branches = [functools.partial(branch, count) for count in COUNTS]
    return lax.switch(which, branches, table, queries, own)


def solution(mesh):
    in_specs = (
        P("tm", "space", None, None, None),
        P("tm", "space", None, None, None),
        P("tm", "space", None, None, None),
        P("tm", "space", None, None),
        P(),
    )
    out_specs = P("tm", "space", None, None, None)
    return jax.shard_map(local, mesh=mesh, in_specs=in_specs, out_specs=out_specs, check_vma=False)
```

```python
import functools

import jax
import jax.numpy as jnp
import numpy as np
from jax import lax
from jax.experimental import pallas as pl
from jax.experimental.pallas import tpu as pltpu
from jax.sharding import PartitionSpec as P

HD = 128
EXPONENT = float(np.log2(np.e) * HD**-0.5)
SLOTS = 9
FRAME_SLOTS = (1, 4, 7)
TILES = 18
ROW = 1 + SLOTS + 2 * TILES
WINDOW = 3
COUNTS = (2, 3, 4, 5, 6, 7, 8, 9, 10, 12)


def head_order(reach):
    heads = reach.shape[0]
    frame, height = reach[:, 0] > 0, reach[:, 1] > 0
    group = jnp.where(height, 0, 2) + jnp.where(frame, 0, 1)
    place = group * heads + jnp.arange(heads, dtype=jnp.int32)
    rank = jnp.sum((place[None, :] < place[:, None]).astype(jnp.int32), axis=1)
    ids = jnp.arange(heads, dtype=jnp.int32)
    order = jnp.sum(jnp.where(rank[:, None] == ids[None, :], ids[:, None], 0), axis=0)
    with_height = jnp.sum(height.astype(jnp.int32))
    return order, with_height


def plan(mask, reach, order, frame_pos, height_pos, frame_count, height_count):
    heads = reach.shape[0]
    tile = np.arange(TILES, dtype=np.int32)
    frame, height = tile // 6 - 1, tile // 2 % 3 - 1
    wide = tile % 2 - np.arange(2, dtype=np.int32)[:, None]
    offset = 9 * (frame + 1) + 3 * (height + 1) + wide + 1
    chosen = (offset[:, :, None] == np.arange(27)).astype(np.int32)
    center = offset == 13
    inside = (frame_pos + frame >= 0) & (frame_pos + frame < frame_count)
    inside = inside & (height_pos + height >= 0) & (height_pos + height < height_count)
    picked = jnp.sum(mask[:, None, :] * chosen, axis=2)
    tile_ok = inside[None, :] & ((picked == 1) | center)
    sorted_reach = reach[order]
    within = np.abs(frame) <= sorted_reach[:, 0:1]
    within = within & (np.abs(height) <= sorted_reach[:, 1:2])
    allow = (
        tile_ok[None] & within[:, None] & (np.abs(wide) <= sorted_reach[:, 2][:, None, None])
    )
    in_slot = (tile // 2 == np.arange(SLOTS)[:, None]).astype(np.int32)
    used = jnp.sum(allow.astype(jnp.int32), axis=1)
    need = (jnp.sum(used[:, None, :] * in_slot, axis=2) > 0).astype(jnp.int32)
    flags = allow.astype(jnp.int32).reshape(heads, 2 * TILES)
    rows = [order[:, None], need, flags]
    return jnp.concatenate(rows, axis=1).reshape(-1)


def pack_kernel(heads, order_ref, key_ref, value_ref, out_ref, sems):
    def copies(head):
        columns = pl.ds(pl.multiple_of(order_ref[head] * HD, HD), HD)
        return [
            pltpu.make_async_copy(
                ref.at[0, 0, :, :, columns], out_ref.at[head, kind], sems.at[kind, head]
            )
            for kind, ref in enumerate((key_ref, value_ref))
        ]

    def begin(head, carry):
        for copy in copies(head):
            copy.start()
        return carry

    def finish(head, carry):
        for copy in copies(head):
            copy.wait()
        return carry

    lax.fori_loop(0, heads, begin, 0)
    lax.fori_loop(0, heads, finish, 0)


def packed(order, keys, values):
    heads = order.shape[0]
    tile_len = keys.shape[3]
    anywhere = pl.BlockSpec(memory_space=pl.ANY)
    return pl.pallas_call(
        functools.partial(pack_kernel, heads),
        out_shape=jax.ShapeDtypeStruct((heads, 2, 2, tile_len, HD), keys.dtype),
        grid_spec=pltpu.PrefetchScalarGridSpec(
            num_scalar_prefetch=1,
            grid=(),
            in_specs=[anywhere, anywhere],
            out_specs=anywhere,
            scratch_shapes=[pltpu.SemaphoreType.DMA((2, heads))],
        ),
    )(order, keys, values)


def exchange_kernel(
    reached,
    frame_count,
    height_count,
    own,
    before,
    after,
    above,
    below,
    above_before,
    above_after,
    below_before,
    below_after,
    frame_send,
    frame_recv,
    side_send,
    side_recv,
    relay_send,
    relay_recv,
):
    frame, height = lax.axis_index("tm"), lax.axis_index("space")
    has_prev, has_next = frame > 0, frame < frame_count - 1
    has_above, has_below = height > 0, height < height_count - 1
    prev, following = (frame - 1, height), (frame + 1, height)
    upper, lower = (frame, height - 1), (frame, height + 1)
    mesh_id = pl.DeviceIdType.MESH
    neighbours = (
        (has_prev, prev),
        (has_next, following),
        (has_above, upper),
        (has_below, lower),
    )

    barrier = pltpu.get_barrier_semaphore()
    for there, device in neighbours:

        @pl.when(there)
        def _():
            pl.semaphore_signal(barrier, inc=1, device_id=device, device_id_type=mesh_id)

    peers = sum(there.astype(jnp.int32) for there, _ in neighbours)
    pl.semaphore_wait(barrier, peers)

    def remote(src, dst, send, recv, device):
        return pltpu.make_async_remote_copy(
            src_ref=src,
            dst_ref=dst,
            send_sem=send,
            recv_sem=recv,
            device_id=device,
            device_id_type=mesh_id,
        )

    def frame_copies():
        return (
            (has_next, has_prev, remote(own, before, frame_send.at[0], frame_recv.at[0], following)),
            (has_prev, has_next, remote(own, after, frame_send.at[1], frame_recv.at[1], prev)),
        )

    def side_copies(j):
        down = remote(own.at[j], above.at[j], side_send.at[0, j], side_recv.at[0, j], lower)
        up = remote(own.at[j], below.at[j], side_send.at[1, j], side_recv.at[1, j], upper)
        return (has_below, has_above, down), (has_above, has_below, up)

    def relay_copies(j):
        made = []
        for k, (src, dst, there, send_to) in enumerate(
            (
                (above, above_before, has_above, True),
                (above, above_after, has_above, False),
                (below, below_before, has_below, True),
                (below, below_after, has_below, False),
            )
        ):
            device = following if send_to else prev
            sends = has_next if send_to else has_prev
            receives = has_prev if send_to else has_next
            copy = remote(src.at[j], dst.at[j], relay_send.at[k, j], relay_recv.at[k, j], device)
            made.append((there & sends, there & receives, copy))
        return made

    def start(copies):
        for sends, _, copy in copies:

            @pl.when(sends)
            def _():
                copy.start()

    def wait_sent(copies):
        for sends, _, copy in copies:

            @pl.when(sends)
            def _():
                copy.wait_send()

    def wait_received(copies):
        for _, receives, copy in copies:

            @pl.when(receives)
            def _():
                copy.wait_recv()

    for j in range(min(WINDOW, reached)):
        start(side_copies(j))
    start(frame_copies())

    def step(j, carry):
        wait_sent(side_copies(j))

        @pl.when(j + WINDOW < reached)
        def _():
            start(side_copies(jnp.minimum(j + WINDOW, reached - 1)))

        wait_received(side_copies(j))
        start(relay_copies(j))
        return carry

    lax.fori_loop(0, reached, step, 0)

    def finish(j, carry):
        wait_sent(relay_copies(j))
        wait_received(relay_copies(j))
        return carry

    wait_sent(frame_copies())
    wait_received(frame_copies())
    lax.fori_loop(0, reached, finish, 0)


def exchanged(reached, own):
    heads = own.shape[0]
    anywhere = pl.BlockSpec(memory_space=pl.ANY)
    full = jax.ShapeDtypeStruct(own.shape, own.dtype)
    some = jax.ShapeDtypeStruct((reached,) + own.shape[1:], own.dtype)
    dma = pltpu.SemaphoreType.DMA
    return pl.pallas_call(
        functools.partial(
            exchange_kernel, reached, lax.axis_size("tm"), lax.axis_size("space")
        ),
        out_shape=[full] * 2 + [some] * 6,
        in_specs=[anywhere],
        out_specs=[anywhere] * 8,
        scratch_shapes=[
            dma((2,)),
            dma((2,)),
            dma((2, reached)),
            dma((2, reached)),
            dma((4, reached)),
            dma((4, reached)),
        ],
        compiler_params=pltpu.CompilerParams(collective_id=reached, has_side_effects=True),
    )(own)


def attend_kernel(heads, tile_len, slots, plan_ref, q_ref, *refs):
    pieces = refs[: len(slots)]
    out_ref, kv, scores, peak, listed, sems = refs[len(slots) :]
    i = pl.program_id(0)
    contract = (((1,), (1,)), ((), ()))

    def transfer(place, buf, begin):
        for ref, slot in zip(pieces, slots):

            @pl.when(plan_ref[place * ROW + 1 + slot] > 0)
            def _():
                copy = pltpu.make_async_copy(
                    ref.at[place], kv.at[buf, slot], sems.at[buf, slot]
                )
                if begin:
                    copy.start()
                else:
                    copy.wait()

    @pl.when(i == 0)
    def _():
        transfer(i, 0, True)

    buf = lax.rem(i, 2)

    @pl.when(i + 1 < heads)
    def _():
        transfer(i + 1, 1 - buf, True)

    transfer(i, buf, False)
    row = i * ROW

    columns = range(2)
    tiles = []
    for c in columns:
        first = row + 1 + SLOTS + c * TILES
        center = TILES // 2 - 1 + c
        for tile in range(TILES + 1):
            listed[c, tile] = center
        count = jnp.int32(0)
        for tile in range(TILES):
            listed[c, count] = tile
            count = count + plan_ref[first + tile]
        listed[c, count] = center
        tiles.append(count)
    pairs = (jnp.maximum(tiles[0], tiles[1]) + 1) // 2
    rows_shape = (tile_len, HD)

    def score(p, largest):
        made = []
        for c in columns:
            best = largest[c]
            for half in range(2):
                tile = listed[c, 2 * p + half]
                part = lax.dot_general(
                    q_ref[0, 0, c],
                    kv[buf, tile // 2, 0, tile % 2],
                    contract,
                    preferred_element_type=jnp.float32,
                )
                part = jnp.where(2 * p + half < tiles[c], part, jnp.float32(-1e30))
                scores[c, p, :, half * tile_len : (half + 1) * tile_len] = part
                for k in range(0, tile_len, HD):
                    best = jnp.maximum(best, part[:, k : k + HD])
            made.append(best)
        return tuple(made)

    lowest = jnp.full(rows_shape, -jnp.inf, jnp.float32)
    largest = lax.fori_loop(0, pairs, score, (lowest, lowest))
    for c in columns:
        peak[c] = jnp.broadcast_to(jnp.max(largest[c], axis=1, keepdims=True), rows_shape)

    def gather(p, state):
        made = []
        for c in columns:
            total, result = state[c]
            rounded = []
            for k in range(0, 2 * tile_len, HD):
                weights = jnp.exp2((scores[c, p, :, k : k + HD] - peak[c]) * EXPONENT)
                total = total + weights
                rounded.append(weights.astype(jnp.bfloat16))
            found = [listed[c, 2 * p + half] for half in range(2)]
            rows = [kv[buf, tile // 2, 1, tile % 2] for tile in found]
            result = result + jnp.dot(
                jnp.concatenate(rounded, axis=1),
                jnp.concatenate(rows, axis=0),
                preferred_element_type=jnp.float32,
            )
            made.append((total, result))
        return tuple(made)

    zero = jnp.zeros(rows_shape, jnp.float32)
    state = lax.fori_loop(0, pairs, gather, ((zero, zero), (zero, zero)))
    for c in columns:
        total = jnp.sum(state[c][0], axis=1, keepdims=True)
        out_ref[0, 0, c] = (state[c][1] / total).astype(jnp.bfloat16)


def attend(table, queries, pieces, heads):
    tile_len = queries.shape[3]
    block = pl.BlockSpec(
        (1, 1, 2, tile_len, HD), lambda i, table: (0, 0, 0, 0, table[i * ROW])
    )
    anywhere = pl.BlockSpec(memory_space=pl.ANY)
    arrays = [array for _, array in pieces]
    slots = tuple(slot for slot, _ in pieces)
    work = heads * 2 * tile_len * TILES * tile_len // 3
    return pl.pallas_call(
        functools.partial(attend_kernel, heads, tile_len, slots),
        out_shape=jax.ShapeDtypeStruct(queries.shape, queries.dtype),
        grid_spec=pltpu.PrefetchScalarGridSpec(
            num_scalar_prefetch=1,
            grid=(heads,),
            in_specs=[block] + [anywhere] * len(arrays),
            out_specs=block,
            scratch_shapes=[
                pltpu.VMEM((2, SLOTS, 2, 2, tile_len, HD), queries.dtype),
                pltpu.VMEM((2, TILES // 2, tile_len, 2 * tile_len), jnp.float32),
                pltpu.VMEM((2, tile_len, HD), jnp.float32),
                pltpu.SMEM((2, TILES + 2), jnp.int32),
                pltpu.SemaphoreType.DMA((2, SLOTS)),
            ],
        ),
        compiler_params=pltpu.CompilerParams(vmem_limit_bytes=60 * 1024 * 1024),
        cost_estimate=pl.CostEstimate(
            flops=work * 4 * HD, bytes_accessed=heads * 2 * 1024 * 1024, transcendentals=work
        ),
    )(table, queries, *arrays)


def branch(reached, table, queries, own):
    heads = own.shape[0]
    arrays = exchanged(reached, own)
    pieces = [(1, arrays[0]), (4, own), (7, arrays[1])]
    pieces += zip((3, 5, 0, 6, 2, 8), arrays[2:])
    return attend(table, queries, pieces, heads)


def local(queries, keys, values, tile_mask, head_reach):
    order, with_height = head_order(head_reach)
    own = packed(order, keys, values)
    table = plan(
        tile_mask[0, 0],
        head_reach,
        order,
        lax.axis_index("tm"),
        lax.axis_index("space"),
        lax.axis_size("tm"),
        lax.axis_size("space"),
    )
    which = jnp.sum((with_height > np.array(COUNTS, np.int32)).astype(jnp.int32))
    branches = [functools.partial(branch, count) for count in COUNTS]
    return lax.switch(which, branches, table, queries, own)


def solution(mesh):
    in_specs = (
        P("tm", "space", None, None, None),
        P("tm", "space", None, None, None),
        P("tm", "space", None, None, None),
        P("tm", "space", None, None),
        P(),
    )
    out_specs = P("tm", "space", None, None, None)
    return jax.shard_map(local, mesh=mesh, in_specs=in_specs, out_specs=out_specs, check_vma=False)
```

```python
import functools

import jax
import jax.numpy as jnp
import numpy as np
from jax import lax
from jax.experimental import pallas as pl
from jax.experimental.pallas import tpu as pltpu
from jax.sharding import PartitionSpec as P

HD = 128
EXPONENT = float(np.log2(np.e) * HD**-0.5)
SLOTS = 9
FRAME_SLOTS = (1, 4, 7)
TILES = 18
ROW = 1 + SLOTS + 2 * TILES
WINDOW = 4
COUNTS = (2, 3, 4, 5, 6, 7, 8, 9, 10, 12)


def head_order(reach):
    heads = reach.shape[0]
    frame, height = reach[:, 0] > 0, reach[:, 1] > 0
    group = jnp.where(height, 0, 2) + jnp.where(frame, 0, 1)
    place = group * heads + jnp.arange(heads, dtype=jnp.int32)
    rank = jnp.sum((place[None, :] < place[:, None]).astype(jnp.int32), axis=1)
    ids = jnp.arange(heads, dtype=jnp.int32)
    order = jnp.sum(jnp.where(rank[:, None] == ids[None, :], ids[:, None], 0), axis=0)
    with_height = jnp.sum(height.astype(jnp.int32))
    return order, with_height


def plan(mask, reach, order, frame_pos, height_pos, frame_count, height_count):
    heads = reach.shape[0]
    tile = np.arange(TILES, dtype=np.int32)
    frame, height = tile // 6 - 1, tile // 2 % 3 - 1
    wide = tile % 2 - np.arange(2, dtype=np.int32)[:, None]
    offset = 9 * (frame + 1) + 3 * (height + 1) + wide + 1
    chosen = (offset[:, :, None] == np.arange(27)).astype(np.int32)
    center = offset == 13
    inside = (frame_pos + frame >= 0) & (frame_pos + frame < frame_count)
    inside = inside & (height_pos + height >= 0) & (height_pos + height < height_count)
    picked = jnp.sum(mask[:, None, :] * chosen, axis=2)
    tile_ok = inside[None, :] & ((picked == 1) | center)
    sorted_reach = reach[order]
    within = np.abs(frame) <= sorted_reach[:, 0:1]
    within = within & (np.abs(height) <= sorted_reach[:, 1:2])
    allow = (
        tile_ok[None] & within[:, None] & (np.abs(wide) <= sorted_reach[:, 2][:, None, None])
    )
    in_slot = (tile // 2 == np.arange(SLOTS)[:, None]).astype(np.int32)
    used = jnp.sum(allow.astype(jnp.int32), axis=1)
    need = (jnp.sum(used[:, None, :] * in_slot, axis=2) > 0).astype(jnp.int32)
    flags = allow.astype(jnp.int32).reshape(heads, 2 * TILES)
    rows = [order[:, None], need, flags]
    return jnp.concatenate(rows, axis=1).reshape(-1)


def pack_kernel(heads, order_ref, key_ref, value_ref, out_ref, sems):
    def copies(head):
        columns = pl.ds(pl.multiple_of(order_ref[head] * HD, HD), HD)
        return [
            pltpu.make_async_copy(
                ref.at[0, 0, :, :, columns], out_ref.at[head, kind], sems.at[kind, head]
            )
            for kind, ref in enumerate((key_ref, value_ref))
        ]

    def begin(head, carry):
        for copy in copies(head):
            copy.start()
        return carry

    def finish(head, carry):
        for copy in copies(head):
            copy.wait()
        return carry

    lax.fori_loop(0, heads, begin, 0)
    lax.fori_loop(0, heads, finish, 0)


def packed(order, keys, values):
    heads = order.shape[0]
    tile_len = keys.shape[3]
    anywhere = pl.BlockSpec(memory_space=pl.ANY)
    return pl.pallas_call(
        functools.partial(pack_kernel, heads),
        out_shape=jax.ShapeDtypeStruct((heads, 2, 2, tile_len, HD), keys.dtype),
        grid_spec=pltpu.PrefetchScalarGridSpec(
            num_scalar_prefetch=1,
            grid=(),
            in_specs=[anywhere, anywhere],
            out_specs=anywhere,
            scratch_shapes=[pltpu.SemaphoreType.DMA((2, heads))],
        ),
    )(order, keys, values)


def exchange_kernel(
    reached,
    frame_count,
    height_count,
    own,
    before,
    after,
    above,
    below,
    above_before,
    above_after,
    below_before,
    below_after,
    frame_send,
    frame_recv,
    side_send,
    side_recv,
    relay_send,
    relay_recv,
):
    frame, height = lax.axis_index("tm"), lax.axis_index("space")
    has_prev, has_next = frame > 0, frame < frame_count - 1
    has_above, has_below = height > 0, height < height_count - 1
    prev, following = (frame - 1, height), (frame + 1, height)
    upper, lower = (frame, height - 1), (frame, height + 1)
    mesh_id = pl.DeviceIdType.MESH
    neighbours = (
        (has_prev, prev),
        (has_next, following),
        (has_above, upper),
        (has_below, lower),
    )

    barrier = pltpu.get_barrier_semaphore()
    for there, device in neighbours:

        @pl.when(there)
        def _():
            pl.semaphore_signal(barrier, inc=1, device_id=device, device_id_type=mesh_id)

    peers = sum(there.astype(jnp.int32) for there, _ in neighbours)
    pl.semaphore_wait(barrier, peers)

    def remote(src, dst, send, recv, device):
        return pltpu.make_async_remote_copy(
            src_ref=src,
            dst_ref=dst,
            send_sem=send,
            recv_sem=recv,
            device_id=device,
            device_id_type=mesh_id,
        )

    def frame_copies():
        return (
            (has_next, has_prev, remote(own, before, frame_send.at[0], frame_recv.at[0], following)),
            (has_prev, has_next, remote(own, after, frame_send.at[1], frame_recv.at[1], prev)),
        )

    def side_copies(j):
        down = remote(own.at[j], above.at[j], side_send.at[0, j], side_recv.at[0, j], lower)
        up = remote(own.at[j], below.at[j], side_send.at[1, j], side_recv.at[1, j], upper)
        return (has_below, has_above, down), (has_above, has_below, up)

    def relay_copies(j):
        made = []
        for k, (src, dst, there, send_to) in enumerate(
            (
                (above, above_before, has_above, True),
                (above, above_after, has_above, False),
                (below, below_before, has_below, True),
                (below, below_after, has_below, False),
            )
        ):
            device = following if send_to else prev
            sends = has_next if send_to else has_prev
            receives = has_prev if send_to else has_next
            copy = remote(src.at[j], dst.at[j], relay_send.at[k, j], relay_recv.at[k, j], device)
            made.append((there & sends, there & receives, copy))
        return made

    def start(copies):
        for sends, _, copy in copies:

            @pl.when(sends)
            def _():
                copy.start()

    def wait_sent(copies):
        for sends, _, copy in copies:

            @pl.when(sends)
            def _():
                copy.wait_send()

    def wait_received(copies):
        for _, receives, copy in copies:

            @pl.when(receives)
            def _():
                copy.wait_recv()

    for j in range(min(WINDOW, reached)):
        start(side_copies(j))
    start(frame_copies())

    def step(j, carry):
        wait_sent(side_copies(j))

        @pl.when(j + WINDOW < reached)
        def _():
            start(side_copies(jnp.minimum(j + WINDOW, reached - 1)))

        wait_received(side_copies(j))
        start(relay_copies(j))
        return carry

    lax.fori_loop(0, reached, step, 0)

    def finish(j, carry):
        wait_sent(relay_copies(j))
        wait_received(relay_copies(j))
        return carry

    wait_sent(frame_copies())
    wait_received(frame_copies())
    lax.fori_loop(0, reached, finish, 0)


def exchanged(reached, own):
    heads = own.shape[0]
    anywhere = pl.BlockSpec(memory_space=pl.ANY)
    full = jax.ShapeDtypeStruct(own.shape, own.dtype)
    some = jax.ShapeDtypeStruct((reached,) + own.shape[1:], own.dtype)
    dma = pltpu.SemaphoreType.DMA
    return pl.pallas_call(
        functools.partial(
            exchange_kernel, reached, lax.axis_size("tm"), lax.axis_size("space")
        ),
        out_shape=[full] * 2 + [some] * 6,
        in_specs=[anywhere],
        out_specs=[anywhere] * 8,
        scratch_shapes=[
            dma((2,)),
            dma((2,)),
            dma((2, reached)),
            dma((2, reached)),
            dma((4, reached)),
            dma((4, reached)),
        ],
        compiler_params=pltpu.CompilerParams(collective_id=reached, has_side_effects=True),
    )(own)


def attend_kernel(heads, tile_len, slots, plan_ref, q_ref, *refs):
    pieces = refs[: len(slots)]
    out_ref, kv, scores, peak, listed, sems = refs[len(slots) :]
    i = pl.program_id(0)
    contract = (((1,), (1,)), ((), ()))

    def transfer(place, buf, begin):
        for ref, slot in zip(pieces, slots):

            @pl.when(plan_ref[place * ROW + 1 + slot] > 0)
            def _():
                copy = pltpu.make_async_copy(
                    ref.at[place], kv.at[buf, slot], sems.at[buf, slot]
                )
                if begin:
                    copy.start()
                else:
                    copy.wait()

    @pl.when(i == 0)
    def _():
        transfer(i, 0, True)

    buf = lax.rem(i, 2)

    @pl.when(i + 1 < heads)
    def _():
        transfer(i + 1, 1 - buf, True)

    transfer(i, buf, False)
    row = i * ROW

    columns = range(2)
    tiles = []
    for c in columns:
        first = row + 1 + SLOTS + c * TILES
        center = TILES // 2 - 1 + c
        for tile in range(TILES + 1):
            listed[c, tile] = center
        count = jnp.int32(0)
        for tile in range(TILES):
            listed[c, count] = tile
            count = count + plan_ref[first + tile]
        listed[c, count] = center
        tiles.append(count)
    pairs = (jnp.maximum(tiles[0], tiles[1]) + 1) // 2
    rows_shape = (tile_len, HD)

    def score(p, largest):
        made = []
        for c in columns:
            best = largest[c]
            for half in range(2):
                tile = listed[c, 2 * p + half]
                part = lax.dot_general(
                    q_ref[0, 0, c],
                    kv[buf, tile // 2, 0, tile % 2],
                    contract,
                    preferred_element_type=jnp.float32,
                )
                part = jnp.where(2 * p + half < tiles[c], part, jnp.float32(-1e30))
                scores[c, p, :, half * tile_len : (half + 1) * tile_len] = part
                for k in range(0, tile_len, HD):
                    best = jnp.maximum(best, part[:, k : k + HD])
            made.append(best)
        return tuple(made)

    lowest = jnp.full(rows_shape, -jnp.inf, jnp.float32)
    largest = lax.fori_loop(0, pairs, score, (lowest, lowest))
    for c in columns:
        peak[c] = jnp.broadcast_to(jnp.max(largest[c], axis=1, keepdims=True), rows_shape)

    def gather(p, state):
        made = []
        for c in columns:
            total, result = state[c]
            rounded = []
            for k in range(0, 2 * tile_len, HD):
                weights = jnp.exp2((scores[c, p, :, k : k + HD] - peak[c]) * EXPONENT)
                total = total + weights
                rounded.append(weights.astype(jnp.bfloat16))
            found = [listed[c, 2 * p + half] for half in range(2)]
            rows = [kv[buf, tile // 2, 1, tile % 2] for tile in found]
            result = result + jnp.dot(
                jnp.concatenate(rounded, axis=1),
                jnp.concatenate(rows, axis=0),
                preferred_element_type=jnp.float32,
            )
            made.append((total, result))
        return tuple(made)

    zero = jnp.zeros(rows_shape, jnp.float32)
    state = lax.fori_loop(0, pairs, gather, ((zero, zero), (zero, zero)))
    for c in columns:
        total = jnp.sum(state[c][0], axis=1, keepdims=True)
        out_ref[0, 0, c] = (state[c][1] / total).astype(jnp.bfloat16)


def attend(table, queries, pieces, heads):
    tile_len = queries.shape[3]
    block = pl.BlockSpec(
        (1, 1, 2, tile_len, HD), lambda i, table: (0, 0, 0, 0, table[i * ROW])
    )
    anywhere = pl.BlockSpec(memory_space=pl.ANY)
    arrays = [array for _, array in pieces]
    slots = tuple(slot for slot, _ in pieces)
    work = heads * 2 * tile_len * TILES * tile_len // 3
    return pl.pallas_call(
        functools.partial(attend_kernel, heads, tile_len, slots),
        out_shape=jax.ShapeDtypeStruct(queries.shape, queries.dtype),
        grid_spec=pltpu.PrefetchScalarGridSpec(
            num_scalar_prefetch=1,
            grid=(heads,),
            in_specs=[block] + [anywhere] * len(arrays),
            out_specs=block,
            scratch_shapes=[
                pltpu.VMEM((2, SLOTS, 2, 2, tile_len, HD), queries.dtype),
                pltpu.VMEM((2, TILES // 2, tile_len, 2 * tile_len), jnp.float32),
                pltpu.VMEM((2, tile_len, HD), jnp.float32),
                pltpu.SMEM((2, TILES + 2), jnp.int32),
                pltpu.SemaphoreType.DMA((2, SLOTS)),
            ],
        ),
        compiler_params=pltpu.CompilerParams(vmem_limit_bytes=60 * 1024 * 1024),
        cost_estimate=pl.CostEstimate(
            flops=work * 4 * HD, bytes_accessed=heads * 2 * 1024 * 1024, transcendentals=work
        ),
    )(table, queries, *arrays)


def branch(reached, table, queries, own):
    heads = own.shape[0]
    arrays = exchanged(reached, own)
    pieces = [(1, arrays[0]), (4, own), (7, arrays[1])]
    pieces += zip((3, 5, 0, 6, 2, 8), arrays[2:])
    return attend(table, queries, pieces, heads)


def local(queries, keys, values, tile_mask, head_reach):
    order, with_height = head_order(head_reach)
    own = packed(order, keys, values)
    table = plan(
        tile_mask[0, 0],
        head_reach,
        order,
        lax.axis_index("tm"),
        lax.axis_index("space"),
        lax.axis_size("tm"),
        lax.axis_size("space"),
    )
    which = jnp.sum((with_height > np.array(COUNTS, np.int32)).astype(jnp.int32))
    branches = [functools.partial(branch, count) for count in COUNTS]
    return lax.switch(which, branches, table, queries, own)


def solution(mesh):
    in_specs = (
        P("tm", "space", None, None, None),
        P("tm", "space", None, None, None),
        P("tm", "space", None, None, None),
        P("tm", "space", None, None),
        P(),
    )
    out_specs = P("tm", "space", None, None, None)
    return jax.shard_map(local, mesh=mesh, in_specs=in_specs, out_specs=out_specs, check_vma=False)
```
